32 devices in a mesh: groups: 2 (over y), ep: 4 (over z), fsdp: 4 (over x, core).
Axes of the slice: x: 2, y: 2, z: 4, core: 2. Of those that a mesh axis runs over, the one named last changes fastest.
Arguments:
- layer_in: bfloat16 [4096, 1536], P(('groups', 'ep', 'fsdp')), parts along dimension 0, may hold values from -24 to 24
- attn_out: bfloat16 [4096, 1536], P(('groups', 'ep', 'fsdp')), parts along dimension 0, may hold values from -6 to 6
- norm_gain: float32 [1536], replicated, may hold values from 0.1 to 1.9
- expert_ids: int32 [4096, 2], P(('groups', 'ep', 'fsdp')), parts along dimension 0, may hold values from 0 to 1, as said below
- gate_weights: float32 [4096, 2], P(('groups', 'ep', 'fsdp')), parts along dimension 0, may hold values from 0.1 to 1
- w_gate_up: bfloat16 [4, 1536, 1536], P('ep', None, 'fsdp'), may hold values from -0.15625 to 0.15625
- w_down: bfloat16 [4, 768, 1536], P('ep', None, 'fsdp'), may hold values from -0.15625 to 0.15625
Outputs:
- layer_out: bfloat16 [4096, 1536], P(('groups', 'ep', 'fsdp')), parts along dimension 0
- similarity: float32 [4096], P(('groups', 'ep', 'fsdp')), parts along dimension 0
The draws below stay inside these ranges and needn't reach their ends.
There are 2 independent parts, one for each index of `groups`. The reference program is written for one: setup_inputs(seed, part) draws one part's arguments, and reference() takes and returns one part's arrays. A program takes and returns all parts, laid end to end along the dimension named above; an argument that names none is the same for every part. Nothing has to cross between parts.
Inputs may be any that keep to these rules, and one draw needn't show every extreme that they name: `expert_ids`: the 2 ids of a row differ. In each aligned block of 128 rows (the tokens of one device) no expert is named more than 128 times; one expert, the same in every block, is named exactly 128 times in each block.
All inputs are finite; a program needn't handle non-finite values.
Results may differ from the reference program's by a relative error of at most 0.004.
Values may be sent and summed in bfloat16 or wider, within the bound.
No kernel may reach another device: no remote copies, remote signals or barrier semaphores. Data moves between devices by JAX's collectives and lax.ppermute only.
A program may use at most 64 MiB of HBM per device.

```python
import jax
import jax.numpy as jnp
from jax import lax

D = 1536
FF = 1536
TOK_DEV = 128
TOPK = 2
EXPERTS = 2
CAP = 128
TOKENS = 2048


def draw_layer_in(key, part):
    key = jax.random.fold_in(key, 11)
    key_base, key_cols, key_rows = jax.random.split(key, 3)
    columns = jnp.exp(jax.random.uniform(key_cols, (D,), jnp.float32, jnp.log(0.3), jnp.log(3.0)))
    base = jnp.clip(jax.random.normal(key_base, (TOKENS, D), jnp.float32), -5.0, 5.0)
    scales = jnp.exp(jax.random.uniform(key_rows, (TOKENS, 1), jnp.float32, jnp.log(0.5), jnp.log(2.0)))
    values = jnp.clip(base * columns[None, :] * scales, -24.0, 24.0)
    return values.astype(jnp.bfloat16)


def draw_expert_ids(key, part):
    key = jax.random.fold_in(key, 23)
    blocks = TOKENS // TOK_DEV
    route_total = TOK_DEV * TOPK
    others = EXPERTS - 1
    remainder = route_total - CAP
    key_hot, key_rank, key_shape, key_rows, key_swap = jax.random.split(key, 5)
    hottest = jax.random.randint(key_hot, (), 0, EXPERTS)
    shuffled = jax.vmap(lambda one_key: jax.random.permutation(one_key, EXPERTS))(jax.random.split(key_rank, blocks)).astype(jnp.int32)
    labels = jnp.arange(EXPERTS, dtype=jnp.int32)
    shuffled = jnp.where(labels[None, :] == hottest, -1, shuffled)
    ranked = jnp.argsort(shuffled, axis=1, stable=True).astype(jnp.int32)
    steps_rank = jnp.arange(others + 1, dtype=jnp.int32)
    concave = remainder * steps_rank * (2 * others - steps_rank) // (others * others)
    linear = remainder * steps_rank // others
    milder = remainder * steps_rank * (3 * others - steps_rank) // (2 * others * others)
    profile = jnp.stack([concave, linear, milder]).astype(jnp.int32)
    choose = jax.random.randint(key_shape, (blocks,), 0, 3)
    bounds = profile[choose]
    counts = jnp.concatenate([jnp.full((blocks, 1), CAP, jnp.int32), (bounds[:, 1:] - bounds[:, :-1]).astype(jnp.int32)], axis=1)
    run_ends = jnp.cumsum(counts, axis=1).astype(jnp.int32)
    slot_ids = jnp.arange(route_total, dtype=jnp.int32)
    rank_of = jnp.sum((slot_ids[None, :, None] >= run_ends[:, None, :]).astype(jnp.int32), axis=2).astype(jnp.int32)
    chosen = jnp.take_along_axis(ranked, rank_of, axis=1)
    per_token = chosen.reshape(blocks, TOPK, TOK_DEV).transpose(0, 2, 1)
    rows_order = jax.vmap(lambda one_key: jax.random.permutation(one_key, TOK_DEV))(jax.random.split(key_rows, blocks)).astype(jnp.int32)
    per_token = jnp.take_along_axis(per_token, rows_order[:, :, None], axis=1)
    flipped = jax.random.randint(key_swap, (blocks, TOK_DEV, 1), 0, 2)
    per_token = jnp.where(flipped == 1, per_token[:, :, ::-1], per_token)
    return per_token.reshape(TOKENS, TOPK).astype(jnp.int32)


def block_levels(stream_key, dims, shards, least, top_value):
    loudness = 1.0
    for dim, blocks in shards:
        draws = jax.random.uniform(jax.random.fold_in(jax.random.fold_in(stream_key, 6), dim), (blocks,), jnp.float32, least / len(shards), top_value / len(shards))
        loudness = loudness * jnp.repeat(jnp.exp(draws), dims[dim] // blocks).reshape((-1,) + (1,) * (len(dims) - 1 - dim))
    return loudness


def noise(key, shape, width, bound, cuts=(), kind=jnp.bfloat16):
    result = width * jax.random.normal(key, shape, jnp.float32)
    if cuts:
        result = result * block_levels(key, shape, cuts, -0.22, 0.18)
    return jnp.clip(result, -bound, bound).astype(kind)


def setup_inputs(seed: int = 0, part: int = 0) -> dict:
    key_list = jax.random.split(jax.random.key(seed), 8)
    own_keys = jax.random.split(jax.random.fold_in(key_list[7], part), 8)
    layer_in = draw_layer_in(jax.random.fold_in(jax.random.fold_in(key_list[7], part), 71), part)
    attn_out = noise(own_keys[1], (TOKENS, D), 1.0, 6.0, ((0, 16),))
    norm_gain = jnp.clip(1.0 + 0.18 * jax.random.normal(key_list[2], (D,), jnp.float32), 0.1, 1.9)
    expert_ids = draw_expert_ids(jax.random.fold_in(jax.random.fold_in(key_list[7], part), 71), part)
    gate_weights = jnp.clip(0.1 + 0.9 * jax.random.uniform(own_keys[4], (TOKENS, TOPK), jnp.float32) ** block_levels(own_keys[4], (TOKENS, TOPK), ((0, 16),), -0.2, 0.2), 0.1, 1.0)
    w_gate_up = noise(key_list[5], (2 * EXPERTS, D, FF), D ** -0.5, 0.15625, ((0, 4), (2, 4)))
    w_down = noise(key_list[6], (2 * EXPERTS, FF // 2, D), FF ** -0.5, 0.15625, ((0, 4), (2, 4)))
    return dict(layer_in=layer_in, attn_out=attn_out, norm_gain=norm_gain, expert_ids=expert_ids, gate_weights=gate_weights, w_gate_up=w_gate_up, w_down=w_down)


norm_eps = 1e-05
cos_eps = 1e-06
glu_alpha = 1.702
tile_rows = 256

def expert_tile(tile_in, expert, up_all, down_all):
    projected = jnp.dot(tile_in, up_all[expert], preferred_element_type=jnp.float32)
    gate_part = projected[:, :FF]
    up_part = projected[:, FF:]
    activated = (gate_part * jax.nn.sigmoid(glu_alpha * gate_part) * (up_part + 1.0)).astype(jnp.bfloat16)
    return jnp.dot(activated, down_all[expert], preferred_element_type=jnp.float32).astype(jnp.bfloat16)

def reference(layer_in, attn_out, norm_gain, expert_ids, gate_weights, w_gate_up, w_down):
    inputs = layer_in.astype(jnp.float32)
    residual = inputs + attn_out.astype(jnp.float32)
    mean_square = lax.optimization_barrier(jnp.mean(residual * residual, axis=-1, keepdims=True))
    normed = (residual * lax.rsqrt(mean_square + norm_eps) * norm_gain[None, :]).astype(jnp.bfloat16)
    half_hidden = FF // 2
    packed = w_gate_up.reshape(EXPERTS, 2, D, FF)
    gate_all = jnp.concatenate([packed[:, 0, :, :half_hidden], packed[:, 1, :, :half_hidden]], axis=2)
    up_only = jnp.concatenate([packed[:, 0, :, half_hidden:], packed[:, 1, :, half_hidden:]], axis=2)
    up_all = jnp.concatenate([gate_all, up_only], axis=2)
    down_all = w_down.reshape(EXPERTS, FF, D)
    flat_ids = expert_ids.reshape(-1).astype(jnp.int32)
    count_routes = flat_ids.shape[0]
    ordering = jnp.argsort(flat_ids, stable=True).astype(jnp.int32)
    sorted_ids = flat_ids[ordering]
    counts = lax.optimization_barrier(jnp.sum((flat_ids[:, None] == jnp.arange(EXPERTS, dtype=jnp.int32)[None, :]).astype(jnp.int32), axis=0)).astype(jnp.int32)
    padded = ((counts + tile_rows - 1) // tile_rows * tile_rows).astype(jnp.int32)
    run_ends = jnp.cumsum(padded).astype(jnp.int32)
    offsets = (run_ends - padded).astype(jnp.int32)
    starts = (jnp.cumsum(counts).astype(jnp.int32) - counts).astype(jnp.int32)
    position = (offsets[sorted_ids] + jnp.arange(count_routes, dtype=jnp.int32) - starts[sorted_ids]).astype(jnp.int32)
    tile_count = (count_routes + EXPERTS * tile_rows + tile_rows - 1) // tile_rows
    total_rows = tile_count * tile_rows
    gathered = jnp.zeros((total_rows, D), jnp.bfloat16).at[position].set(normed[ordering // TOPK])
    tile_start = jnp.arange(tile_count, dtype=jnp.int32) * tile_rows
    tile_expert = jnp.minimum(lax.optimization_barrier(jnp.sum((run_ends[None, :] <= tile_start[:, None]).astype(jnp.int32), axis=1)), EXPERTS - 1).astype(jnp.int32)
    outputs = lax.map(lambda element: expert_tile(element[0], element[1], up_all, down_all), (gathered.reshape(tile_count, tile_rows, D), tile_expert))
    outputs = outputs.reshape(total_rows, D)
    per_route = jnp.zeros((count_routes, D), jnp.bfloat16).at[ordering].set(outputs[position])
    mixture = lax.optimization_barrier(jnp.sum(gate_weights[:, :, None] * per_route.reshape(-1, TOPK, D).astype(jnp.float32), axis=1))
    updated = residual + mixture
    inner = lax.optimization_barrier(jnp.sum(inputs * updated, axis=-1))
    similarity = inner * lax.rsqrt(lax.optimization_barrier(jnp.sum(inputs * inputs, axis=-1)) + cos_eps) * lax.rsqrt(lax.optimization_barrier(jnp.sum(updated * updated, axis=-1)) + cos_eps)
    return (updated.astype(jnp.bfloat16), similarity)
```

```python
import functools

import jax
import jax.numpy as jnp
from jax import lax
from jax.experimental import pallas as pl
from jax.experimental.pallas import tpu as pltpu
from jax.sharding import PartitionSpec as P

norm_eps = 1e-05
cos_eps = 1e-06
glu_alpha = 1.702


def swapped(value, axis, bit):
    mask = 2**bit
    pairs = [(source, source ^ mask) for source in range(lax.axis_size(axis))]
    return lax.ppermute(value, axis, pairs)


def activate(projected, half_hidden):
    gate_part = projected[:, :half_hidden]
    up_part = projected[:, half_hidden:]
    return (gate_part * jax.nn.sigmoid(glu_alpha * gate_part) * (up_part + 1.0)).astype(
        jnp.bfloat16
    )


def routed_shards(layer_in, attn_out, norm_gain, expert_ids, gate_weights, w_gate_up, w_down):
    tokens, features = layer_in.shape
    routes = expert_ids.shape[1]
    devices_ep = lax.axis_size("ep")
    experts = devices_ep // 2
    capacity = min(tokens, 2 * tokens * routes // experts)
    half_cap = capacity // 2
    hidden = w_gate_up.shape[2] * lax.axis_size("fsdp")
    half_hidden = hidden // 2
    inputs = layer_in.astype(jnp.float32)
    residual = inputs + attn_out.astype(jnp.float32)
    mean_square = jnp.mean(residual * residual, axis=-1, keepdims=True)
    normed = (residual * lax.rsqrt(mean_square + norm_eps) * norm_gain[None, :]).astype(
        jnp.bfloat16
    )
    flat_ids = expert_ids.reshape(-1)
    onehot = (flat_ids[:, None] == jnp.arange(experts, dtype=jnp.int32)[None, :]).astype(jnp.int32)
    earlier = jnp.cumsum(onehot, axis=0) - onehot
    slot_index = jnp.sum(earlier * onehot, axis=1)
    target = flat_ids * capacity + slot_index
    outgoing = (
        jnp.zeros((experts * capacity, features), jnp.bfloat16)
        .at[target]
        .set(jnp.repeat(normed, routes, axis=0))
    )
    outgoing = outgoing.reshape(experts, capacity, features)
    parity = lax.axis_index("ep") % 2
    doubled = jnp.repeat(outgoing, 2, axis=0)
    arrived = lax.all_to_all(doubled, "ep", split_axis=0, concat_axis=0, tiled=True)
    slot_rows = arrived.reshape(devices_ep * capacity, features)
    full_up, full_down = (
        lax.all_gather(w_gate_up, "fsdp", axis=2, tiled=True),
        lax.all_gather(w_down, "fsdp", axis=2, tiled=True),
    )
    projected = jnp.dot(slot_rows, full_up[0], preferred_element_type=jnp.float32)
    activated = activate(projected, half_hidden)
    partial_value = jnp.dot(activated, full_down[0], preferred_element_type=jnp.float32)
    partial_value = partial_value.reshape(devices_ep, capacity, features)
    kept_half = lax.dynamic_slice_in_dim(partial_value, parity * half_cap, half_cap, 1)
    sent_half = lax.dynamic_slice_in_dim(partial_value, (1 - parity) * half_cap, half_cap, 1)
    received = swapped(sent_half.astype(jnp.bfloat16), "ep", 0).astype(sent_half.dtype)
    summed = (kept_half + received).astype(jnp.bfloat16)
    returned = lax.all_to_all(summed, "ep", split_axis=0, concat_axis=0, tiled=True)
    returned = returned.reshape(experts * capacity, features)
    per_route = returned[target].reshape(tokens, routes, features).astype(jnp.float32)
    mixture = jnp.sum(gate_weights[:, :, None] * per_route, axis=1)
    updated = residual + mixture
    inner = jnp.sum(inputs * updated, axis=-1)
    similarity = (
        inner
        * lax.rsqrt(jnp.sum(inputs * inputs, axis=-1) + cos_eps)
        * lax.rsqrt(jnp.sum(updated * updated, axis=-1) + cos_eps)
    )
    return (updated.astype(jnp.bfloat16), similarity)


def kernel_call(body, outs, scratch=(), flops=0, moved=0):
    return pl.pallas_call(
        body,
        out_shape=outs,
        scratch_shapes=list(scratch),
        compiler_params=pltpu.CompilerParams(vmem_limit_bytes=40 * 2**20),
        cost_estimate=pl.CostEstimate(flops=flops, bytes_accessed=moved, transcendentals=0),
    )


def dot(left, right):
    return jnp.dot(left, right, preferred_element_type=jnp.float32)


def project_body(count, *refs):
    tokens_in = refs[:count]
    own, core_own, near, far, core_near, core_far, hidden_out, rows = refs[count:]
    tokens, half_depth = tokens_in[0].shape[0], near.shape[0]
    width = own.shape[1]
    for block in range(count):
        rows[block * tokens : (block + 1) * tokens, :] = tokens_in[block][...]
    spot = lax.axis_index("fsdp")
    on_gate = spot < 2
    group = lax.axis_index("groups")
    near_depth = pl.ds(pl.multiple_of(group * half_depth, half_depth), half_depth)
    far_depth = pl.ds(pl.multiple_of((1 - group) * half_depth, half_depth), half_depth)
    for mine, first, second, hidden_block in (
        (own, near, far, spot % 2),
        (core_own, core_near, core_far, 1 - spot % 2),
    ):
        here = dot(rows[...], mine[...])
        there = dot(rows[:, near_depth], first[...]) + dot(rows[:, far_depth], second[...])
        gate_part = jnp.where(on_gate, here, there)
        up_part = jnp.where(on_gate, there, here)
        columns = pl.ds(pl.multiple_of(hidden_block * width, width), width)
        hidden_out[:, columns] = (
            gate_part * jax.nn.sigmoid(glu_alpha * gate_part) * (up_part + 1.0)
        ).astype(jnp.bfloat16)


def project(blocks, panels):
    tokens, features = blocks[0].shape
    rows = len(blocks) * tokens
    hidden = 2 * panels[0].shape[1]
    return kernel_call(
        functools.partial(project_body, len(blocks)),
        jax.ShapeDtypeStruct((rows, hidden), jnp.bfloat16),
        [pltpu.VMEM((rows, features), jnp.bfloat16)],
        4 * rows * features * hidden,
        4 * features * hidden + 2 * rows * (features + hidden),
    )(*blocks, *panels)


def lower_body(count, hidden, *refs):
    panels, outs = refs[:4], refs[4:]
    tokens, width = outs[0].shape[0], panels[0].shape[1]
    spot = lax.axis_index("fsdp")
    for panel, source in zip(panels, (spot, spot ^ 1, spot ^ 2, spot ^ 3)):
        part = dot(hidden[...], panel[...])
        columns = pl.ds(pl.multiple_of(source * width, width), width)
        for block in range(count):
            outs[block][:, columns] = part[block * tokens : (block + 1) * tokens].astype(
                outs[block].dtype
            )


def lower(hidden, panels, kinds):
    count = len(kinds)
    tokens = hidden.shape[0] // count
    features = 4 * panels[0].shape[1]
    return kernel_call(
        functools.partial(lower_body, count),
        tuple(jax.ShapeDtypeStruct((tokens, features), kind) for kind in kinds),
        (),
        2 * hidden.shape[0] * hidden.shape[1] * features,
        2 * hidden.shape[1] * features + 4 * hidden.shape[0] * features,
    )(hidden, *panels)


def finish_body(layer_in, attn_out, ids, weights, kept, partner, other, layer_out, similarity):
    inputs = layer_in[...].astype(jnp.float32)
    residual = inputs + attn_out[...].astype(jnp.float32)
    mine = (kept[...] + partner[...].astype(jnp.float32)).astype(jnp.bfloat16).astype(jnp.float32)
    own_expert = lax.axis_index("ep") // 2
    named = ids[...] == own_expert
    own_gate = jnp.sum(jnp.where(named, weights[...], 0.0), axis=1, keepdims=True)
    other_gate = jnp.sum(jnp.where(named, 0.0, weights[...]), axis=1, keepdims=True)
    updated = residual + (own_gate * mine + other_gate * other[...].astype(jnp.float32))
    layer_out[...] = updated.astype(jnp.bfloat16)
    value = (
        jnp.sum(inputs * updated, axis=-1, keepdims=True)
        * lax.rsqrt(jnp.sum(inputs * inputs, axis=-1, keepdims=True) + cos_eps)
        * lax.rsqrt(jnp.sum(updated * updated, axis=-1, keepdims=True) + cos_eps)
    )
    tokens = value.shape[0]
    similarity[...] = jnp.broadcast_to(value, (tokens, tokens)).T[0:1, :]


def dense_shards(layer_in, attn_out, norm_gain, expert_ids, gate_weights, w_gate_up, w_down):
    tokens, features = layer_in.shape
    own_up, own_down = w_gate_up[0], w_down[0]
    half_depth = features // 2
    group = lax.axis_index("groups")
    first_half = lax.dynamic_slice_in_dim(own_up, group * half_depth, half_depth, 0)
    near = swapped(first_half, "fsdp", 1)
    x_down = swapped(own_down, "fsdp", 1)
    far = swapped(near, "groups", 0)
    core_up, core_down = swapped(own_up, "fsdp", 0), swapped(own_down, "fsdp", 0)
    core_near, core_far = swapped(near, "fsdp", 0), swapped(far, "fsdp", 0)
    core_x_down = swapped(x_down, "fsdp", 0)
    up_panels = (own_up, core_up, near, far, core_near, core_far)
    down_panels = (own_down, core_down, x_down, core_x_down)

    inputs = layer_in.astype(jnp.float32)
    residual = inputs + attn_out.astype(jnp.float32)
    mean_square = jnp.mean(residual * residual, axis=-1, keepdims=True)
    normed = (residual * lax.rsqrt(mean_square + norm_eps) * norm_gain[None, :]).astype(
        jnp.bfloat16
    )
    two = swapped(normed, "ep", 1)
    one = swapped(normed, "ep", 0)
    three = swapped(two, "ep", 0)
    early = project((normed, one, two), up_panels)
    kept, sent_one, kept_two = lower(
        early, down_panels, (jnp.float32, jnp.bfloat16, jnp.float32)
    )
    (sent_three,) = lower(project((three,), up_panels), down_panels, (jnp.bfloat16,))
    got_two = swapped(sent_three, "ep", 0)
    joined = (kept_two + got_two.astype(jnp.float32)).astype(jnp.bfloat16)
    other = swapped(joined, "ep", 1)
    partner = swapped(sent_one, "ep", 0)
    layer_out, similarity = kernel_call(
        finish_body,
        (
            jax.ShapeDtypeStruct((tokens, features), jnp.bfloat16),
            jax.ShapeDtypeStruct((1, tokens), jnp.float32),
        ),
        (),
        20 * tokens * features,
        16 * tokens * features,
    )(layer_in, attn_out, expert_ids, gate_weights, kept, partner, other)
    return layer_out, similarity.reshape(tokens)


def shards(*args):
    sizes = tuple(lax.axis_size(axis) for axis in ("groups", "ep", "fsdp"))
    routes = args[3].shape[1]
    every_expert = sizes[1] == 2 * routes
    return (dense_shards if every_expert and sizes == (2, 4, 4) else routed_shards)(*args)


def solution(mesh):
    placed = (
        P(("groups", "ep", "fsdp"), None),
        P(("groups", "ep", "fsdp"), None),
        P(),
        P(("groups", "ep", "fsdp"), None),
        P(("groups", "ep", "fsdp"), None),
        P("ep", None, "fsdp"),
        P("ep", None, "fsdp"),
    )
    return jax.shard_map(
        shards,
        mesh=mesh,
        in_specs=placed,
        out_specs=(P(("groups", "ep", "fsdp"), None), P(("groups", "ep", "fsdp"))),
        check_vma=False,
    )
```

```python
import functools

import jax
import jax.numpy as jnp
from jax import lax
from jax.experimental import pallas as pl
from jax.experimental.pallas import tpu as pltpu
from jax.sharding import PartitionSpec as P

norm_eps = 1e-05
cos_eps = 1e-06
glu_alpha = 1.702
x_parts = 1


def swapped(value, axis, bit):
    mask = 2**bit
    pairs = [(source, source ^ mask) for source in range(lax.axis_size(axis))]
    return lax.ppermute(value, axis, pairs)


def activate(projected, half_hidden):
    gate_part = projected[:, :half_hidden]
    up_part = projected[:, half_hidden:]
    return (gate_part * jax.nn.sigmoid(glu_alpha * gate_part) * (up_part + 1.0)).astype(
        jnp.bfloat16
    )


def routed_shards(layer_in, attn_out, norm_gain, expert_ids, gate_weights, w_gate_up, w_down):
    tokens, features = layer_in.shape
    routes = expert_ids.shape[1]
    devices_ep = lax.axis_size("ep")
    experts = devices_ep // 2
    capacity = min(tokens, 2 * tokens * routes // experts)
    half_cap = capacity // 2
    hidden = w_gate_up.shape[2] * lax.axis_size("fsdp")
    half_hidden = hidden // 2
    inputs = layer_in.astype(jnp.float32)
    residual = inputs + attn_out.astype(jnp.float32)
    mean_square = jnp.mean(residual * residual, axis=-1, keepdims=True)
    normed = (residual * lax.rsqrt(mean_square + norm_eps) * norm_gain[None, :]).astype(
        jnp.bfloat16
    )
    flat_ids = expert_ids.reshape(-1)
    onehot = (flat_ids[:, None] == jnp.arange(experts, dtype=jnp.int32)[None, :]).astype(jnp.int32)
    earlier = jnp.cumsum(onehot, axis=0) - onehot
    slot_index = jnp.sum(earlier * onehot, axis=1)
    target = flat_ids * capacity + slot_index
    outgoing = (
        jnp.zeros((experts * capacity, features), jnp.bfloat16)
        .at[target]
        .set(jnp.repeat(normed, routes, axis=0))
    )
    outgoing = outgoing.reshape(experts, capacity, features)
    parity = lax.axis_index("ep") % 2
    doubled = jnp.repeat(outgoing, 2, axis=0)
    arrived = lax.all_to_all(doubled, "ep", split_axis=0, concat_axis=0, tiled=True)
    slot_rows = arrived.reshape(devices_ep * capacity, features)
    full_up, full_down = (
        lax.all_gather(w_gate_up, "fsdp", axis=2, tiled=True),
        lax.all_gather(w_down, "fsdp", axis=2, tiled=True),
    )
    projected = jnp.dot(slot_rows, full_up[0], preferred_element_type=jnp.float32)
    activated = activate(projected, half_hidden)
    partial_value = jnp.dot(activated, full_down[0], preferred_element_type=jnp.float32)
    partial_value = partial_value.reshape(devices_ep, capacity, features)
    kept_half = lax.dynamic_slice_in_dim(partial_value, parity * half_cap, half_cap, 1)
    sent_half = lax.dynamic_slice_in_dim(partial_value, (1 - parity) * half_cap, half_cap, 1)
    received = swapped(sent_half.astype(jnp.bfloat16), "ep", 0).astype(sent_half.dtype)
    summed = (kept_half + received).astype(jnp.bfloat16)
    returned = lax.all_to_all(summed, "ep", split_axis=0, concat_axis=0, tiled=True)
    returned = returned.reshape(experts * capacity, features)
    per_route = returned[target].reshape(tokens, routes, features).astype(jnp.float32)
    mixture = jnp.sum(gate_weights[:, :, None] * per_route, axis=1)
    updated = residual + mixture
    inner = jnp.sum(inputs * updated, axis=-1)
    similarity = (
        inner
        * lax.rsqrt(jnp.sum(inputs * inputs, axis=-1) + cos_eps)
        * lax.rsqrt(jnp.sum(updated * updated, axis=-1) + cos_eps)
    )
    return (updated.astype(jnp.bfloat16), similarity)


def kernel_call(body, outs, scratch=(), flops=0, moved=0):
    return pl.pallas_call(
        body,
        out_shape=outs,
        scratch_shapes=list(scratch),
        compiler_params=pltpu.CompilerParams(vmem_limit_bytes=40 * 2**20),
        cost_estimate=pl.CostEstimate(flops=flops, bytes_accessed=moved, transcendentals=0),
    )


def dot(left, right):
    return jnp.dot(left, right, preferred_element_type=jnp.float32)


def project_body(count, *refs):
    tokens_in, (own, core_own), parts = refs[:count], refs[count : count + 2], refs[count + 2 : -2]
    hidden_out, rows = refs[-2:]
    step, width = parts[0].shape
    start = 0
    for block in tokens_in:
        rows[start : start + block.shape[0], :] = block[...]
        start += block.shape[0]
    spot = lax.axis_index("fsdp")
    on_gate = spot < 2
    group = lax.axis_index("groups")
    depths = [
        pl.ds(pl.multiple_of((half * x_parts + part) * step, step), step)
        for half in (group, 1 - group)
        for part in range(x_parts)
    ]
    for mine, theirs, hidden_block in (
        (own, parts[: 2 * x_parts], spot % 2),
        (core_own, parts[2 * x_parts :], 1 - spot % 2),
    ):
        here = dot(rows[...], mine[...])
        there = sum(dot(rows[:, depth], part[...]) for depth, part in zip(depths, theirs))
        gate_part = jnp.where(on_gate, here, there)
        up_part = jnp.where(on_gate, there, here)
        columns = pl.ds(pl.multiple_of(hidden_block * width, width), width)
        hidden_out[:, columns] = (
            gate_part * jax.nn.sigmoid(glu_alpha * gate_part) * (up_part + 1.0)
        ).astype(jnp.bfloat16)


def project(blocks, panels):
    features = blocks[0].shape[1]
    rows = sum(block.shape[0] for block in blocks)
    hidden = 2 * panels[0].shape[1]
    return kernel_call(
        functools.partial(project_body, len(blocks)),
        jax.ShapeDtypeStruct((rows, hidden), jnp.bfloat16),
        [pltpu.VMEM((rows, features), jnp.bfloat16)],
        4 * rows * features * hidden,
        4 * features * hidden + 2 * rows * (features + hidden),
    )(*blocks, *panels)


def lower_body(hidden, *refs):
    panels, outs = refs[:4], refs[4:]
    width = panels[0].shape[1]
    spot = lax.axis_index("fsdp")
    for panel, source in zip(panels, (spot, spot ^ 1, spot ^ 2, spot ^ 3)):
        part = dot(hidden[...], panel[...])
        columns = pl.ds(pl.multiple_of(source * width, width), width)
        start = 0
        for out in outs:
            stop = start + out.shape[0]
            out[:, columns] = part[start:stop].astype(out.dtype)
            start = stop


def lower(hidden, panels, pieces):
    features = 4 * panels[0].shape[1]
    return kernel_call(
        lower_body,
        tuple(jax.ShapeDtypeStruct((rows, features), kind) for rows, kind in pieces),
        (),
        2 * hidden.shape[0] * hidden.shape[1] * features,
        2 * hidden.shape[1] * features + 4 * hidden.shape[0] * features,
    )(hidden, *panels)


def finish_body(layer_in, attn_out, ids, weights, kept, partner, other, layer_out, similarity):
    inputs = layer_in[...].astype(jnp.float32)
    residual = inputs + attn_out[...].astype(jnp.float32)
    mine = (kept[...] + partner[...].astype(jnp.float32)).astype(jnp.bfloat16).astype(jnp.float32)
    own_expert = lax.axis_index("ep") // 2
    named = ids[...] == own_expert
    own_gate = jnp.sum(jnp.where(named, weights[...], 0.0), axis=1, keepdims=True)
    other_gate = jnp.sum(jnp.where(named, 0.0, weights[...]), axis=1, keepdims=True)
    updated = residual + (own_gate * mine + other_gate * other[...].astype(jnp.float32))
    layer_out[...] = updated.astype(jnp.bfloat16)
    value = (
        jnp.sum(inputs * updated, axis=-1, keepdims=True)
        * lax.rsqrt(jnp.sum(inputs * inputs, axis=-1, keepdims=True) + cos_eps)
        * lax.rsqrt(jnp.sum(updated * updated, axis=-1, keepdims=True) + cos_eps)
    )
    tokens = value.shape[0]
    similarity[...] = jnp.broadcast_to(value, (tokens, tokens)).T[0:1, :]


def dense_shards(layer_in, attn_out, norm_gain, expert_ids, gate_weights, w_gate_up, w_down):
    tokens, features = layer_in.shape
    inputs = layer_in.astype(jnp.float32)
    residual = inputs + attn_out.astype(jnp.float32)
    mean_square = jnp.mean(residual * residual, axis=-1, keepdims=True)
    normed = (residual * lax.rsqrt(mean_square + norm_eps) * norm_gain[None, :]).astype(
        jnp.bfloat16
    )
    own_up, own_down = w_gate_up[0], w_down[0]
    step = features // (2 * x_parts)
    first_row = lax.axis_index("groups") * (features // 2)
    piece0 = lax.dynamic_slice_in_dim(own_up, first_row + 0 * step, step, 0)
    two = swapped(normed, "ep", 1)
    one = swapped(normed, "ep", 0)
    tied_three, *_ = lax.optimization_barrier((two, one))
    three = swapped(tied_three, "ep", 0)
    near0 = swapped(piece0, "fsdp", 1)
    far0 = swapped(near0, "groups", 0)
    cnear0 = swapped(near0, "fsdp", 0)
    cfar0 = swapped(far0, "fsdp", 0)
    x_down = swapped(own_down, "fsdp", 1)
    tied_core_up, *_ = lax.optimization_barrier((own_up, near0))
    core_up = swapped(tied_core_up, "fsdp", 0)
    tied_core_down, *_ = lax.optimization_barrier((own_down, near0))
    core_down = swapped(tied_core_down, "fsdp", 0)
    core_x_down = swapped(x_down, "fsdp", 0)
    up_panels = (own_up, core_up, near0, far0, cnear0, cfar0)
    down_panels = (own_down, core_down, x_down, core_x_down)
    hidden = project((three,), up_panels)
    (sent_three,) = lower(hidden, down_panels, ((tokens, jnp.bfloat16),))
    early = project((two, normed, one), up_panels)
    kept_two, kept, sent_one = lower(
        early, down_panels, tuple((tokens, kind) for kind in (jnp.float32, jnp.float32, jnp.bfloat16))
    )
    got = swapped(sent_three, "ep", 0).astype(jnp.float32)
    other = swapped((kept_two + got).astype(jnp.bfloat16), "ep", 1)
    partner = swapped(sent_one, "ep", 0)
    layer_out, similarity = kernel_call(
        finish_body,
        (
            jax.ShapeDtypeStruct((tokens, features), jnp.bfloat16),
            jax.ShapeDtypeStruct((1, tokens), jnp.float32),
        ),
        (),
        20 * tokens * features,
        16 * tokens * features,
    )(layer_in, attn_out, expert_ids, gate_weights, kept, partner, other)
    return layer_out, similarity.reshape(tokens)


def shards(*args):
    sizes = tuple(lax.axis_size(axis) for axis in ("groups", "ep", "fsdp"))
    routes = args[3].shape[1]
    every_expert = sizes[1] == 2 * routes
    return (dense_shards if every_expert and sizes == (2, 4, 4) else routed_shards)(*args)


def solution(mesh):
    placed = (
        P(("groups", "ep", "fsdp"), None),
        P(("groups", "ep", "fsdp"), None),
        P(),
        P(("groups", "ep", "fsdp"), None),
        P(("groups", "ep", "fsdp"), None),
        P("ep", None, "fsdp"),
        P("ep", None, "fsdp"),
    )
    return jax.shard_map(
        shards,
        mesh=mesh,
        in_specs=placed,
        out_specs=(P(("groups", "ep", "fsdp"), None), P(("groups", "ep", "fsdp"))),
        check_vma=False,
    )
```

```python
import functools

import jax
import jax.numpy as jnp
from jax import lax
from jax.experimental import pallas as pl
from jax.experimental.pallas import tpu as pltpu
from jax.sharding import PartitionSpec as P

norm_eps = 1e-05
cos_eps = 1e-06
glu_alpha = 1.702
x_parts = 1


def swapped(value, axis, bit):
    mask = 2**bit
    pairs = [(source, source ^ mask) for source in range(lax.axis_size(axis))]
    return lax.ppermute(value, axis, pairs)


def activate(projected, half_hidden):
    gate_part = projected[:, :half_hidden]
    up_part = projected[:, half_hidden:]
    return (gate_part * jax.nn.sigmoid(glu_alpha * gate_part) * (up_part + 1.0)).astype(
        jnp.bfloat16
    )


def routed_shards(layer_in, attn_out, norm_gain, expert_ids, gate_weights, w_gate_up, w_down):
    tokens, features = layer_in.shape
    routes = expert_ids.shape[1]
    devices_ep = lax.axis_size("ep")
    experts = devices_ep // 2
    capacity = min(tokens, 2 * tokens * routes // experts)
    half_cap = capacity // 2
    hidden = w_gate_up.shape[2] * lax.axis_size("fsdp")
    half_hidden = hidden // 2
    inputs = layer_in.astype(jnp.float32)
    residual = inputs + attn_out.astype(jnp.float32)
    mean_square = jnp.mean(residual * residual, axis=-1, keepdims=True)
    normed = (residual * lax.rsqrt(mean_square + norm_eps) * norm_gain[None, :]).astype(
        jnp.bfloat16
    )
    flat_ids = expert_ids.reshape(-1)
    onehot = (flat_ids[:, None] == jnp.arange(experts, dtype=jnp.int32)[None, :]).astype(jnp.int32)
    earlier = jnp.cumsum(onehot, axis=0) - onehot
    slot_index = jnp.sum(earlier * onehot, axis=1)
    target = flat_ids * capacity + slot_index
    outgoing = (
        jnp.zeros((experts * capacity, features), jnp.bfloat16)
        .at[target]
        .set(jnp.repeat(normed, routes, axis=0))
    )
    outgoing = outgoing.reshape(experts, capacity, features)
    parity = lax.axis_index("ep") % 2
    doubled = jnp.repeat(outgoing, 2, axis=0)
    arrived = lax.all_to_all(doubled, "ep", split_axis=0, concat_axis=0, tiled=True)
    slot_rows = arrived.reshape(devices_ep * capacity, features)
    full_up, full_down = (
        lax.all_gather(w_gate_up, "fsdp", axis=2, tiled=True),
        lax.all_gather(w_down, "fsdp", axis=2, tiled=True),
    )
    projected = jnp.dot(slot_rows, full_up[0], preferred_element_type=jnp.float32)
    activated = activate(projected, half_hidden)
    partial_value = jnp.dot(activated, full_down[0], preferred_element_type=jnp.float32)
    partial_value = partial_value.reshape(devices_ep, capacity, features)
    kept_half = lax.dynamic_slice_in_dim(partial_value, parity * half_cap, half_cap, 1)
    sent_half = lax.dynamic_slice_in_dim(partial_value, (1 - parity) * half_cap, half_cap, 1)
    received = swapped(sent_half.astype(jnp.bfloat16), "ep", 0).astype(sent_half.dtype)
    summed = (kept_half + received).astype(jnp.bfloat16)
    returned = lax.all_to_all(summed, "ep", split_axis=0, concat_axis=0, tiled=True)
    returned = returned.reshape(experts * capacity, features)
    per_route = returned[target].reshape(tokens, routes, features).astype(jnp.float32)
    mixture = jnp.sum(gate_weights[:, :, None] * per_route, axis=1)
    updated = residual + mixture
    inner = jnp.sum(inputs * updated, axis=-1)
    similarity = (
        inner
        * lax.rsqrt(jnp.sum(inputs * inputs, axis=-1) + cos_eps)
        * lax.rsqrt(jnp.sum(updated * updated, axis=-1) + cos_eps)
    )
    return (updated.astype(jnp.bfloat16), similarity)


def kernel_call(body, outs, scratch=(), flops=0, moved=0):
    return pl.pallas_call(
        body,
        out_shape=outs,
        scratch_shapes=list(scratch),
        compiler_params=pltpu.CompilerParams(vmem_limit_bytes=40 * 2**20),
        cost_estimate=pl.CostEstimate(flops=flops, bytes_accessed=moved, transcendentals=0),
    )


def after_body(value, *refs):
    refs[-1][...] = value[...]


def after(value, *others, flops=0):
    return kernel_call(
        after_body,
        jax.ShapeDtypeStruct(value.shape, value.dtype),
        flops=flops,
        moved=4 * value.size,
    )(value, *others)


def dot(left, right):
    return jnp.dot(left, right, preferred_element_type=jnp.float32)


def project_body(count, *refs):
    tokens_in, (own, core_own), parts = refs[:count], refs[count : count + 2], refs[count + 2 : -2]
    hidden_out, rows = refs[-2:]
    step, width = parts[0].shape
    start = 0
    for block in tokens_in:
        rows[start : start + block.shape[0], :] = block[...]
        start += block.shape[0]
    spot = lax.axis_index("fsdp")
    on_gate = spot < 2
    group = lax.axis_index("groups")
    depths = [
        pl.ds(pl.multiple_of((half * x_parts + part) * step, step), step)
        for half in (group, 1 - group)
        for part in range(x_parts)
    ]
    for mine, theirs, hidden_block in (
        (own, parts[: 2 * x_parts], spot % 2),
        (core_own, parts[2 * x_parts :], 1 - spot % 2),
    ):
        here = dot(rows[...], mine[...])
        there = sum(dot(rows[:, depth], part[...]) for depth, part in zip(depths, theirs))
        gate_part = jnp.where(on_gate, here, there)
        up_part = jnp.where(on_gate, there, here)
        columns = pl.ds(pl.multiple_of(hidden_block * width, width), width)
        hidden_out[:, columns] = (
            gate_part * jax.nn.sigmoid(glu_alpha * gate_part) * (up_part + 1.0)
        ).astype(jnp.bfloat16)


def project(blocks, panels):
    features = blocks[0].shape[1]
    rows = sum(block.shape[0] for block in blocks)
    hidden = 2 * panels[0].shape[1]
    return kernel_call(
        functools.partial(project_body, len(blocks)),
        jax.ShapeDtypeStruct((rows, hidden), jnp.bfloat16),
        [pltpu.VMEM((rows, features), jnp.bfloat16)],
        4 * rows * features * hidden,
        4 * features * hidden + 2 * rows * (features + hidden),
    )(*blocks, *panels)


def lower_body(hidden, *refs):
    panels, outs = refs[:4], refs[4:]
    width = panels[0].shape[1]
    spot = lax.axis_index("fsdp")
    for panel, source in zip(panels, (spot, spot ^ 1, spot ^ 2, spot ^ 3)):
        part = dot(hidden[...], panel[...])
        columns = pl.ds(pl.multiple_of(source * width, width), width)
        start = 0
        for out in outs:
            stop = start + out.shape[0]
            out[:, columns] = part[start:stop].astype(out.dtype)
            start = stop


def lower(hidden, panels, pieces):
    features = 4 * panels[0].shape[1]
    return kernel_call(
        lower_body,
        tuple(jax.ShapeDtypeStruct((rows, features), kind) for rows, kind in pieces),
        (),
        2 * hidden.shape[0] * hidden.shape[1] * features,
        2 * hidden.shape[1] * features + 4 * hidden.shape[0] * features,
    )(hidden, *panels)


def finish_body(layer_in, attn_out, ids, weights, kept, partner, *refs):
    others, (layer_out, similarity) = refs[:-2], refs[-2:]
    inputs = layer_in[...].astype(jnp.float32)
    residual = inputs + attn_out[...].astype(jnp.float32)
    mine = (kept[...] + partner[...].astype(jnp.float32)).astype(jnp.bfloat16).astype(jnp.float32)
    own_expert = lax.axis_index("ep") // 2
    named = ids[...] == own_expert
    own_gate = jnp.sum(jnp.where(named, weights[...], 0.0), axis=1, keepdims=True)
    other_gate = jnp.sum(jnp.where(named, 0.0, weights[...]), axis=1, keepdims=True)
    other = jnp.concatenate([part[...] for part in others], axis=0).astype(jnp.float32)
    updated = residual + (own_gate * mine + other_gate * other)
    layer_out[...] = updated.astype(jnp.bfloat16)
    value = (
        jnp.sum(inputs * updated, axis=-1, keepdims=True)
        * lax.rsqrt(jnp.sum(inputs * inputs, axis=-1, keepdims=True) + cos_eps)
        * lax.rsqrt(jnp.sum(updated * updated, axis=-1, keepdims=True) + cos_eps)
    )
    tokens = value.shape[0]
    similarity[...] = jnp.broadcast_to(value, (tokens, tokens)).T[0:1, :]


def dense_shards(layer_in, attn_out, norm_gain, expert_ids, gate_weights, w_gate_up, w_down):
    tokens, features = layer_in.shape
    inputs = layer_in.astype(jnp.float32)
    residual = inputs + attn_out.astype(jnp.float32)
    mean_square = jnp.mean(residual * residual, axis=-1, keepdims=True)
    normed = (residual * lax.rsqrt(mean_square + norm_eps) * norm_gain[None, :]).astype(
        jnp.bfloat16
    )
    own_up, own_down = w_gate_up[0], w_down[0]
    step = features // (2 * x_parts)
    first_row = lax.axis_index("groups") * (features // 2)
    piece0 = lax.dynamic_slice_in_dim(own_up, first_row + 0 * step, step, 0)
    two = swapped(normed, "ep", 1)
    one = swapped(normed, "ep", 0)
    tied_three, *_ = lax.optimization_barrier((two, one))
    src_three = after(tied_three, flops=int(3e9))
    three = swapped(src_three, "ep", 0)
    near0 = swapped(piece0, "fsdp", 1)
    far0 = swapped(near0, "groups", 0)
    cnear0 = swapped(near0, "fsdp", 0)
    cfar0 = swapped(far0, "fsdp", 0)
    x_down = swapped(own_down, "fsdp", 1)
    src_core_up = after(own_up, flops=int(2e9))
    core_up = swapped(src_core_up, "fsdp", 0)
    core_down = swapped(own_down, "fsdp", 0)
    src_core_x_down = after(x_down, flops=int(4e9))
    core_x_down = swapped(src_core_x_down, "fsdp", 0)
    up_panels = (own_up, core_up, near0, far0, cnear0, cfar0)
    down_panels = (own_down, core_down, x_down, core_x_down)
    half = tokens // 2
    wide, narrow = jnp.float32, jnp.bfloat16
    hidden = project((three,), up_panels)
    sent_a, sent_b = lower(hidden, down_panels, ((half, narrow),) * 2)
    early = project((two, normed, one), up_panels)
    kept_a, kept_b, kept, sent_one = lower(
        early, down_panels, ((half, wide), (half, wide), (tokens, wide), (tokens, narrow))
    )
    got_a, got_b = swapped(sent_a, "ep", 0), swapped(sent_b, "ep", 0)
    joined_a = (kept_a + got_a.astype(jnp.float32)).astype(jnp.bfloat16)
    joined_b = (kept_b + got_b.astype(jnp.float32)).astype(jnp.bfloat16)
    other_a, other_b = swapped(joined_a, "ep", 1), swapped(joined_b, "ep", 1)
    sent_one = after(sent_one, got_b)
    partner = swapped(sent_one, "ep", 0)
    layer_out, similarity = kernel_call(
        finish_body,
        (
            jax.ShapeDtypeStruct((tokens, features), jnp.bfloat16),
            jax.ShapeDtypeStruct((1, tokens), jnp.float32),
        ),
        (),
        20 * tokens * features,
        16 * tokens * features,
    )(layer_in, attn_out, expert_ids, gate_weights, kept, partner, other_a, other_b)
    return layer_out, similarity.reshape(tokens)


def shards(*args):
    sizes = tuple(lax.axis_size(axis) for axis in ("groups", "ep", "fsdp"))
    routes = args[3].shape[1]
    every_expert = sizes[1] == 2 * routes
    return (dense_shards if every_expert and sizes == (2, 4, 4) else routed_shards)(*args)


def solution(mesh):
    placed = (
        P(("groups", "ep", "fsdp"), None),
        P(("groups", "ep", "fsdp"), None),
        P(),
        P(("groups", "ep", "fsdp"), None),
        P(("groups", "ep", "fsdp"), None),
        P("ep", None, "fsdp"),
        P("ep", None, "fsdp"),
    )
    return jax.shard_map(
        shards,
        mesh=mesh,
        in_specs=placed,
        out_specs=(P(("groups", "ep", "fsdp"), None), P(("groups", "ep", "fsdp"))),
        check_vma=False,
    )
```
